32 devices in a mesh: lon: 8 (over y, x, core), lat: 4 (over z).
Axes of the slice: x: 2, y: 2, z: 4, core: 2. Of those that a mesh axis runs over, the one named last changes fastest.
Arguments:
- tracers: bfloat16 [12, 64, 32, 1024], P(None, None, 'lat', 'lon'), may hold values from 0.099609375 to 2
- east_wind: bfloat16 [64, 32, 1024], P(None, 'lat', 'lon'), may hold values from -0.44921875 to 0.44921875
- north_wind: bfloat16 [64, 32, 1024], P(None, 'lat', 'lon'), may hold values from -0.44921875 to 0.44921875
- sunlit: int32 [32, 1024], P('lat', 'lon'), may hold values from 0 to 1, as said below
- coupling: float32 [12, 12], replicated, may hold values from -0.15 to 0.15
- rate_table: float32 [8, 64], replicated, may hold values from 0.01 to 0.6
- rate_index: int32 [12], replicated, may hold values from 0 to 7
- kappa: float32 [63], replicated, may hold values from 0.05 to 0.24
Outputs:
- updated: bfloat16 [12, 64, 32, 1024], P(None, None, 'lat', 'lon')
The draws below stay inside these ranges and needn't reach their ends.
Inputs may be any that keep to these rules, and one draw needn't show every extreme that they name: A device's block of columns holds at most 768 sunlit columns, and together with the block of the device half the lon axis away (same lat index) at most 1024; both bounds are reached in every draw.
All inputs are finite; a program needn't handle non-finite values.
Results may differ from the reference program's by a relative error of at most 0.001.
Values may be sent and summed in bfloat16 or wider, within the bound.
A program may use at most 128 MiB of HBM per device.

```python
import math
import jax
import jax.numpy as jnp
from jax import lax

S = 12
LEV = 64
CLON = 128
CLAT = 8
SUBSTEPS = 16
RATES = 8
COLS = 1024
NLON = 1024
NLAT = 32
LON_TILES = 8
LAT_TILES = 4


def draw_sunlit(key, part):
    paired = LON_TILES // 2
    key_lead, key_rest, key_side, key_rank = jax.random.split(jax.random.fold_in(key, 11), 4)
    quarter = COLS // 4
    leading = jax.random.randint(key_lead, (LAT_TILES, paired), quarter, 3 * quarter + 1)
    leftover = COLS - leading
    trailing = jax.random.randint(key_rest, (LAT_TILES, paired), 0, leftover + 1)
    leading = leading.at[0, 0].set(3 * quarter)
    trailing = trailing.at[0, 0].set(quarter)
    sided = jax.random.randint(key_side, (LAT_TILES, paired), 0, 2)
    western = jnp.where(sided == 1, leading, trailing)
    eastern = jnp.where(sided == 1, trailing, leading)
    counted = jnp.concatenate([western, eastern], axis=1)
    scores = jax.random.randint(key_rank, (LAT_TILES, LON_TILES, COLS), 0, 2 ** 16) * COLS
    scores = scores + jnp.arange(COLS, dtype=jnp.int32)[None, None, :]
    ranking = jnp.argsort(jnp.argsort(scores, axis=-1), axis=-1)
    lit = (ranking < counted[:, :, None]).astype(jnp.int32)
    lit = lit.reshape(LAT_TILES, LON_TILES, CLAT, CLON).transpose(0, 2, 1, 3)
    return lit.reshape(NLAT, NLON)


def set_ends(entries, rng, smallest, high):
    place = [jax.random.randint(jax.random.fold_in(rng, axis), (), 0, length) for axis, length in enumerate(entries.shape)]
    widest = entries.shape.index(max(entries.shape))
    beside = place[:widest] + [(place[widest] + 1) % entries.shape[widest]] + place[widest + 1:]
    return entries.at[tuple(place)].set(smallest).at[tuple(beside)].set(high)


def block_scale(own_key, dims, pieces, smallest, top_value):
    gain = 1.0
    for axis_at, shards_of in pieces:
        draws = jax.random.uniform(jax.random.fold_in(jax.random.fold_in(own_key, 6), axis_at), (shards_of,), jnp.float32, smallest / len(pieces), top_value / len(pieces))
        gain = gain * jnp.repeat(jnp.exp(draws), dims[axis_at] // shards_of).reshape((-1,) + (1,) * (len(dims) - 1 - axis_at))
    return gain


def noise(own_key, extent, deviation, reach, held_as=jnp.bfloat16):
    entries = deviation * jax.random.normal(own_key, extent, jnp.float32)
    return jnp.clip(entries, min=-reach, max=reach).astype(held_as)


def setup_inputs(seed: int = 0) -> dict:
    arg_keys = jax.random.split(jax.random.key(seed), 9)
    tracers = jnp.clip(0.099609375 + 1.9003906 * jax.random.uniform(arg_keys[0], (S, LEV, NLAT, NLON), jnp.float32) ** block_scale(arg_keys[0], (S, LEV, NLAT, NLON), ((2, 4), (3, 8)), -0.2, 0.2), 0.099609375, 2.0).astype(jnp.bfloat16)
    east_wind = jnp.clip(jax.random.uniform(arg_keys[1], (LEV, NLAT, NLON), jnp.float32, -0.44921875, 0.44921875) * block_scale(arg_keys[1], (LEV, NLAT, NLON), ((1, 4), (2, 8)), -0.4, 0.0), -0.44921875, 0.44921875).astype(jnp.bfloat16)
    north_wind = jnp.clip(jax.random.uniform(arg_keys[2], (LEV, NLAT, NLON), jnp.float32, -0.44921875, 0.44921875) * block_scale(arg_keys[2], (LEV, NLAT, NLON), ((1, 4), (2, 8)), -0.4, 0.0), -0.44921875, 0.44921875).astype(jnp.bfloat16)
    sunlit = draw_sunlit(jax.random.fold_in(arg_keys[8], 71), 0)
    coupling = noise(arg_keys[4], (S, S), 0.03, 0.15, jnp.float32)
    rate_table = jnp.clip(jnp.exp(jax.random.uniform(arg_keys[5], (RATES, LEV), jnp.float32, math.log(0.01), math.log(0.6))), 0.01, 0.6)
    rate_index = set_ends(jax.random.randint(arg_keys[6], (S,), 0, RATES), jax.random.fold_in(arg_keys[6], 1), 0, RATES - 1).astype(jnp.int32)
    kappa = jnp.clip(jax.random.uniform(arg_keys[7], (LEV - 1,), jnp.float32, 0.05, 0.24), 0.05, 0.24)
    return {"tracers": tracers, "east_wind": east_wind, "north_wind": north_wind, "sunlit": sunlit, "coupling": coupling, "rate_table": rate_table, "rate_index": rate_index, "kappa": kappa}


def chemistry(start, coupling, loss, kappa):
    state = start.astype(jnp.float32)

    def substep(step, state):
        made = jnp.einsum('st,tlk->slk', coupling, state, precision=lax.Precision.HIGHEST)
        state = (state + made) / (1.0 + loss[:, :, None] * (1.0 + state * state))
        flux = kappa[None, :, None] * (state[:, 1:] - state[:, :-1])
        zeros = jnp.zeros_like(flux[:, :1])
        return state + jnp.concatenate([flux, zeros], axis=1) - jnp.concatenate([zeros, flux], axis=1)

    return lax.fori_loop(0, SUBSTEPS, substep, state)


def advect_species(inputs):
    conc, speed_east, speed_north = inputs
    west_cell = jnp.roll(conc, 1, axis=2)
    west_flux = jnp.maximum(speed_east, 0.0) * west_cell + jnp.minimum(speed_east, 0.0) * conc
    east_flux = jnp.roll(west_flux, -1, axis=2)
    zero_row = jnp.zeros_like(conc[:, :1])
    south_cell = jnp.concatenate([zero_row, conc[:, :-1]], axis=1)
    south_flux = jnp.maximum(speed_north, 0.0) * south_cell + jnp.minimum(speed_north, 0.0) * conc
    north_flux = jnp.concatenate([south_flux[:, 1:], zero_row], axis=1)
    return (conc - (east_flux - west_flux) - (north_flux - south_flux)).astype(jnp.bfloat16)


def reference(tracers, east_wind, north_wind, sunlit, coupling, rate_table, rate_index, kappa):
    speed_east = east_wind.astype(jnp.float32)
    speed_north = north_wind.astype(jnp.float32).at[:, 0, :].set(0.0)
    advected = lax.map(lambda conc: advect_species((conc.astype(jnp.float32), speed_east, speed_north)), tracers)
    loss = rate_table[rate_index]
    blocked = advected.reshape(S, LEV, LAT_TILES, CLAT * NLON).transpose(2, 0, 1, 3)
    light = sunlit.reshape(LAT_TILES, CLAT * NLON)

    def one_block(inputs):
        block, lit = inputs
        finished = chemistry(block, coupling, loss, kappa).astype(jnp.bfloat16)
        return jnp.where(lit[None, None, :] > 0, finished, block)

    result = lax.map(one_block, (blocked, light))
    return result.transpose(1, 2, 0, 3).reshape(S, LEV, NLAT, NLON)
```

```python
import jax
import jax.numpy as jnp
from jax import lax
from jax.experimental import pallas as pl
from jax.experimental.pallas import tpu as pltpu
from jax.sharding import PartitionSpec as P

SUBSTEPS = 16
CHUNK = 8
F32 = jnp.float32
BF16 = jnp.bfloat16
MESH = pl.DeviceIdType.MESH


def rims_kernel(
    lon_count,
    lat_count,
    c_ref,
    u_ref,
    v_ref,
    west_ref,
    east_ref,
    south_ref,
    north_ref,
    wide,
    to_east,
    to_west,
    to_north,
    to_south,
    send_sem,
    recv_sem,
):
    species, levels, rows, cols = c_ref.shape
    lon, lat = lax.axis_index("lon"), lax.axis_index("lat")
    east, west = lax.rem(lon + 1, lon_count), lax.rem(lon + lon_count - 1, lon_count)
    has_south, has_north = lat > 0, lat < lat_count - 1

    barrier = pltpu.get_barrier_semaphore()
    for side in (east, west):
        pl.semaphore_signal(barrier, inc=1, device_id=(side, lat), device_id_type=MESH)

    @pl.when(has_south)
    def _():
        pl.semaphore_signal(barrier, inc=1, device_id=(lon, lat - 1), device_id_type=MESH)

    @pl.when(has_north)
    def _():
        pl.semaphore_signal(barrier, inc=1, device_id=(lon, lat + 1), device_id_type=MESH)

    def widen(s, _):
        wide[pl.ds(s * levels, levels)] = c_ref[s].astype(F32)
        return 0

    lax.fori_loop(0, species, widen, 0)
    wide[pl.ds(species * levels, levels)] = v_ref[...].astype(F32)
    to_south[...] = wide[:, 0, :].astype(BF16)
    to_north[...] = wide[: species * levels, rows - 1, :].astype(BF16)

    peers = 2 + jnp.where(has_south, 1, 0) + jnp.where(has_north, 1, 0)
    pl.semaphore_wait(barrier, peers)

    send_south = pltpu.make_async_remote_copy(
        src_ref=to_south,
        dst_ref=north_ref,
        send_sem=send_sem.at[0],
        recv_sem=recv_sem.at[0],
        device_id=(lon, lat - 1),
        device_id_type=MESH,
    )
    send_north = pltpu.make_async_remote_copy(
        src_ref=to_north,
        dst_ref=south_ref,
        send_sem=send_sem.at[1],
        recv_sem=recv_sem.at[1],
        device_id=(lon, lat + 1),
        device_id_type=MESH,
    )

    @pl.when(has_south)
    def _():
        send_south.start()

    @pl.when(has_north)
    def _():
        send_north.start()

    lane = lax.broadcasted_iota(jnp.int32, (rows, cols), 1)
    wide[pl.ds(species * levels, levels)] = u_ref[...].astype(F32)

    def pack(s, _):
        last = jnp.zeros((rows, cols), F32)
        first = jnp.zeros((rows, cols), F32)
        for k in range(levels):
            turned = pltpu.roll(wide[s * levels + k], (k + 1) % cols, 1)
            last = jnp.where(lane == k, turned, last)
            first = jnp.where(lane == k + 1, turned, first)
        to_east[s] = last
        to_west[s] = first
        return 0

    lax.fori_loop(0, species + 1, pack, 0)
    send_east = pltpu.make_async_remote_copy(
        src_ref=to_east,
        dst_ref=west_ref,
        send_sem=send_sem.at[2],
        recv_sem=recv_sem.at[2],
        device_id=(east, lat),
        device_id_type=MESH,
    )
    send_west = pltpu.make_async_remote_copy(
        src_ref=to_west,
        dst_ref=east_ref,
        send_sem=send_sem.at[3],
        recv_sem=recv_sem.at[3],
        device_id=(west, lat),
        device_id_type=MESH,
    )
    send_east.start()
    send_west.start()

    @pl.when(jnp.logical_not(has_south))
    def _():
        south_ref[...] = jnp.zeros_like(south_ref)

    @pl.when(jnp.logical_not(has_north))
    def _():
        north_ref[...] = jnp.zeros_like(north_ref)

    send_east.wait()
    send_west.wait()

    @pl.when(has_south)
    def _():
        send_south.wait_send()
        send_north.wait_recv()

    @pl.when(has_north)
    def _():
        send_north.wait_send()
        send_south.wait_recv()


def column_kernel(
    coupling_ref,
    table_ref,
    index_ref,
    kappa_ref,
    c_ref,
    u_ref,
    v_ref,
    light_ref,
    west_ref,
    east_ref,
    south_ref,
    north_ref,
    out_ref,
    state,
    loss,
    base,
    matrix_wide,
    matrix,
    south,
    north,
):
    species, levels, rows, cols = c_ref.shape
    mix = species * rows
    pairs = levels // 2
    lane = lax.broadcasted_iota(jnp.int32, (rows, cols), 1)
    sub = lax.broadcasted_iota(jnp.int32, (rows, cols), 0)

    col = lax.broadcasted_iota(jnp.int32, (rows, 4 * mix), 1)
    row = lax.broadcasted_iota(jnp.int32, (rows, 4 * mix), 0)
    place = lax.rem(col, mix)
    for s in range(species):
        value = jnp.zeros((rows, 4 * mix), F32)
        for t in range(species):
            entry = coupling_ref[s, t] + (1.0 if s == t else 0.0)
            value = jnp.where(place == row + t * rows, entry, value)
        high = value.astype(BF16).astype(F32)
        matrix_wide[s * rows : (s + 1) * rows, :] = jnp.where(
            col < 2 * mix, high, value - high
        )
    matrix[...] = matrix_wide[...].astype(BF16)
    south[...] = south_ref[...].astype(F32)
    north[...] = north_ref[...].astype(F32)
    at_wall = jnp.logical_and(lax.axis_index("lat") == 0, sub == 0)

    def advect(p, _):
        for half in range(2):
            k = 2 * p + half
            lanes = slice(half * cols, (half + 1) * cols)
            u = u_ref[k].astype(F32)
            v = jnp.where(at_wall, 0.0, v_ref[k].astype(F32))
            to_first = lax.rem(cols - k, cols)
            to_last = cols - 2 - k
            u_east = jnp.where(
                lane == cols - 1,
                pltpu.roll(east_ref[species], to_last, 1),
                pltpu.roll(u, cols - 1, 1),
            )
            v_north = jnp.where(
                sub == rows - 1,
                north[pl.ds(species * levels + k, 1), :],
                pltpu.roll(v, rows - 1, 0),
            )
            from_west, to_west = jnp.maximum(u, 0.0), jnp.minimum(u, 0.0)
            to_east, from_east = jnp.maximum(u_east, 0.0), jnp.minimum(u_east, 0.0)
            from_south, to_south = jnp.maximum(v, 0.0), jnp.minimum(v, 0.0)
            to_north, from_north = jnp.maximum(v_north, 0.0), jnp.minimum(v_north, 0.0)
            stay = 1.0 - (to_east - to_west) - (to_north - to_south)
            for s in range(species):
                c = c_ref[s, k].astype(F32)
                c_west = jnp.where(
                    lane == 0, pltpu.roll(west_ref[s], to_first, 1), pltpu.roll(c, 1, 1)
                )
                c_east = jnp.where(
                    lane == cols - 1,
                    pltpu.roll(east_ref[s], to_last, 1),
                    pltpu.roll(c, cols - 1, 1),
                )
                c_south = jnp.where(
                    sub == 0, south[pl.ds(s * levels + k, 1), :], pltpu.roll(c, 1, 0)
                )
                c_north = jnp.where(
                    sub == rows - 1,
                    north[pl.ds(s * levels + k, 1), :],
                    pltpu.roll(c, rows - 1, 0),
                )
                value = (
                    stay * c
                    + (from_west * c_west - from_east * c_east)
                    + (from_south * c_south - from_north * c_north)
                ).astype(BF16)
                out_ref[s, k] = value
                tile = slice(s * rows, (s + 1) * rows)
                state[p + 1, tile, lanes] = value.astype(F32)
                rate = table_ref[index_ref[s], k]
                loss[p, tile, lanes] = jnp.full((rows, cols), rate, F32)
                base[p, tile, lanes] = jnp.full((rows, cols), 1.0 + rate, F32)
        return 0

    lax.fori_loop(0, pairs, advect, 0)

    def substep(step, _):
        def chunk(b, carry):
            below, flux = carry
            for i in range(CHUNK):
                p = b * CHUNK + i
                q = state[p + 1]
                high = q.astype(BF16)
                low = (q - high.astype(F32)).astype(BF16)
                made = jnp.dot(
                    matrix[...],
                    jnp.concatenate([high, low, high, low], axis=0),
                    preferred_element_type=F32,
                )
                under = base[p] + loss[p] * (q * q)
                guess = pl.reciprocal(under, approx=True)
                z = (made * guess) * (2.0 - under * guess)
                for half in range(2):
                    here = z[:, half * cols : (half + 1) * cols]
                    k = 2 * p + half
                    rate = jnp.where(k > 0, kappa_ref[jnp.maximum(k - 1, 0)], 0.0)
                    upward = rate * (here - below)
                    lanes = slice((1 - half) * cols, (2 - half) * cols)
                    state[p + half, :, lanes] = below + (upward - flux)
                    below, flux = here, upward
            return below, flux

        zero = jnp.zeros((mix, cols), F32)
        below, flux = lax.fori_loop(0, pairs // CHUNK, chunk, (zero, zero))
        state[pairs, :, cols:] = below - flux
        return 0

    lax.fori_loop(0, SUBSTEPS, substep, 0)

    lit = light_ref[...] > 0

    def finish(p, _):
        for half in range(2):
            k = 2 * p + half
            lanes = slice(half * cols, (half + 1) * cols)
            for s in range(species):
                done = state[p + 1, s * rows : (s + 1) * rows, lanes]
                out_ref[s, k] = jnp.where(lit, done, out_ref[s, k].astype(F32)).astype(BF16)
        return 0

    lax.fori_loop(0, pairs, finish, 0)


def vmem():
    return pl.BlockSpec(memory_space=pltpu.VMEM)


def smem():
    return pl.BlockSpec(memory_space=pltpu.SMEM)


def solution(mesh):
    placed = (
        P(None, None, "lat", "lon"),
        P(None, "lat", "lon"),
        P(None, "lat", "lon"),
        P("lat", "lon"),
        P(),
        P(),
        P(),
        P(),
    )
    lon_count, lat_count = mesh.shape["lon"], mesh.shape["lat"]

    def local(tracers, east_wind, north_wind, sunlit, coupling, rate_table, rate_index, kappa):
        species, levels, rows, cols = tracers.shape
        mix = species * rows
        pairs = levels // 2

        def rims(*refs):
            return rims_kernel(lon_count, lat_count, *refs)

        sides = pl.pallas_call(
            rims,
            out_shape=(
                jax.ShapeDtypeStruct((species + 1, rows, cols), F32),
                jax.ShapeDtypeStruct((species + 1, rows, cols), F32),
                jax.ShapeDtypeStruct((species * levels, cols), BF16),
                jax.ShapeDtypeStruct(((species + 1) * levels, cols), BF16),
            ),
            in_specs=[vmem()] * 3,
            out_specs=(vmem(),) * 4,
            scratch_shapes=[
                pltpu.VMEM(((species + 1) * levels, rows, cols), F32),
                pltpu.VMEM((species + 1, rows, cols), F32),
                pltpu.VMEM((species + 1, rows, cols), F32),
                pltpu.VMEM((species * levels, cols), BF16),
                pltpu.VMEM(((species + 1) * levels, cols), BF16),
                pltpu.SemaphoreType.DMA((4,)),
                pltpu.SemaphoreType.DMA((4,)),
            ],
            compiler_params=pltpu.CompilerParams(
                collective_id=0, has_side_effects=True, vmem_limit_bytes=32 * 2**20
            ),
            name="rims",
        )(tracers, east_wind, north_wind)
        return pl.pallas_call(
            column_kernel,
            out_shape=jax.ShapeDtypeStruct(tracers.shape, BF16),
            in_specs=[smem()] * 4 + [vmem()] * 8,
            out_specs=vmem(),
            scratch_shapes=[
                pltpu.VMEM((pairs + 1, mix, 2 * cols), F32),
                pltpu.VMEM((pairs, mix, 2 * cols), F32),
                pltpu.VMEM((pairs, mix, 2 * cols), F32),
                pltpu.VMEM((mix, 4 * mix), F32),
                pltpu.VMEM((mix, 4 * mix), BF16),
                pltpu.VMEM((species * levels, cols), F32),
                pltpu.VMEM(((species + 1) * levels, cols), F32),
            ],
            compiler_params=pltpu.CompilerParams(vmem_limit_bytes=40 * 2**20),
            name="columns",
        )(
            coupling,
            rate_table,
            rate_index,
            kappa,
            tracers,
            east_wind,
            north_wind,
            sunlit,
            *sides,
        )

    return jax.shard_map(
        local, mesh=mesh, in_specs=placed, out_specs=P(None, None, "lat", "lon"), check_vma=False
    )
```

```python
import jax
import jax.numpy as jnp
from jax import lax
from jax.experimental import pallas as pl
from jax.experimental.pallas import tpu as pltpu
from jax.sharding import PartitionSpec as P

SUBSTEPS = 16
F32 = jnp.float32
BF16 = jnp.bfloat16
MESH = pl.DeviceIdType.MESH


def rims_kernel(
    lon_count,
    lat_count,
    c_ref,
    u_ref,
    v_ref,
    west_ref,
    east_ref,
    south_ref,
    north_ref,
    wide,
    to_east,
    to_west,
    to_north,
    to_south,
    send_sem,
    recv_sem,
):
    species, levels, rows, cols = c_ref.shape
    lon, lat = lax.axis_index("lon"), lax.axis_index("lat")
    east, west = lax.rem(lon + 1, lon_count), lax.rem(lon + lon_count - 1, lon_count)
    has_south, has_north = lat > 0, lat < lat_count - 1

    barrier = pltpu.get_barrier_semaphore()
    for side in (east, west):
        pl.semaphore_signal(barrier, inc=1, device_id=(side, lat), device_id_type=MESH)

    @pl.when(has_south)
    def _():
        pl.semaphore_signal(barrier, inc=1, device_id=(lon, lat - 1), device_id_type=MESH)

    @pl.when(has_north)
    def _():
        pl.semaphore_signal(barrier, inc=1, device_id=(lon, lat + 1), device_id_type=MESH)

    def widen(s, _):
        wide[pl.ds(s * levels, levels)] = c_ref[s].astype(F32)
        return 0

    lax.fori_loop(0, species, widen, 0)
    wide[pl.ds(species * levels, levels)] = v_ref[...].astype(F32)
    to_south[...] = wide[:, 0, :].astype(BF16)
    to_north[...] = wide[: species * levels, rows - 1, :].astype(BF16)

    peers = 2 + jnp.where(has_south, 1, 0) + jnp.where(has_north, 1, 0)
    pl.semaphore_wait(barrier, peers)

    send_south = pltpu.make_async_remote_copy(
        src_ref=to_south,
        dst_ref=north_ref,
        send_sem=send_sem.at[0],
        recv_sem=recv_sem.at[0],
        device_id=(lon, lat - 1),
        device_id_type=MESH,
    )
    send_north = pltpu.make_async_remote_copy(
        src_ref=to_north,
        dst_ref=south_ref,
        send_sem=send_sem.at[1],
        recv_sem=recv_sem.at[1],
        device_id=(lon, lat + 1),
        device_id_type=MESH,
    )

    @pl.when(has_south)
    def _():
        send_south.start()

    @pl.when(has_north)
    def _():
        send_north.start()

    lane = lax.broadcasted_iota(jnp.int32, (rows, cols), 1)
    wide[pl.ds(species * levels, levels)] = u_ref[...].astype(F32)

    def pack(s, _):
        last = jnp.zeros((rows, cols), F32)
        first = jnp.zeros((rows, cols), F32)
        for k in range(levels):
            turned = pltpu.roll(wide[s * levels + k], (k + 1) % cols, 1)
            last = jnp.where(lane == k, turned, last)
            first = jnp.where(lane == k + 1, turned, first)
        to_east[s] = last
        to_west[s] = first
        return 0

    lax.fori_loop(0, species + 1, pack, 0)
    send_east = pltpu.make_async_remote_copy(
        src_ref=to_east,
        dst_ref=west_ref,
        send_sem=send_sem.at[2],
        recv_sem=recv_sem.at[2],
        device_id=(east, lat),
        device_id_type=MESH,
    )
    send_west = pltpu.make_async_remote_copy(
        src_ref=to_west,
        dst_ref=east_ref,
        send_sem=send_sem.at[3],
        recv_sem=recv_sem.at[3],
        device_id=(west, lat),
        device_id_type=MESH,
    )
    send_east.start()
    send_west.start()

    @pl.when(jnp.logical_not(has_south))
    def _():
        south_ref[...] = jnp.zeros_like(south_ref)

    @pl.when(jnp.logical_not(has_north))
    def _():
        north_ref[...] = jnp.zeros_like(north_ref)

    send_east.wait()
    send_west.wait()

    @pl.when(has_south)
    def _():
        send_south.wait_send()
        send_north.wait_recv()

    @pl.when(has_north)
    def _():
        send_north.wait_send()
        send_south.wait_recv()


def column_kernel(
    coupling_ref,
    table_ref,
    index_ref,
    kappa_ref,
    c_ref,
    u_ref,
    v_ref,
    light_ref,
    west_ref,
    east_ref,
    south_ref,
    north_ref,
    out_ref,
    state,
    loss,
    base,
    matrix_wide,
    matrix,
    south,
    north,
):
    species, levels, rows, cols = c_ref.shape
    mix = species * rows
    pairs = levels // 2
    lane = lax.broadcasted_iota(jnp.int32, (rows, cols), 1)
    sub = lax.broadcasted_iota(jnp.int32, (rows, cols), 0)

    col = lax.broadcasted_iota(jnp.int32, (rows, 4 * mix), 1)
    row = lax.broadcasted_iota(jnp.int32, (rows, 4 * mix), 0)
    place = lax.rem(col, mix)
    for s in range(species):
        value = jnp.zeros((rows, 4 * mix), F32)
        for t in range(species):
            entry = coupling_ref[s, t] + (1.0 if s == t else 0.0)
            value = jnp.where(place == row + t * rows, entry, value)
        high = value.astype(BF16).astype(F32)
        matrix_wide[s * rows : (s + 1) * rows, :] = jnp.where(
            col < 2 * mix, high, value - high
        )
    matrix[...] = matrix_wide[...].astype(BF16)
    south[...] = south_ref[...].astype(F32)
    north[...] = north_ref[...].astype(F32)
    at_wall = jnp.logical_and(lax.axis_index("lat") == 0, sub == 0)

    def advect(p, _):
        for half in range(2):
            k = 2 * p + half
            lanes = slice(half * cols, (half + 1) * cols)
            u = u_ref[k].astype(F32)
            v = jnp.where(at_wall, 0.0, v_ref[k].astype(F32))
            to_first = lax.rem(cols - k, cols)
            to_last = cols - 2 - k
            u_east = jnp.where(
                lane == cols - 1,
                pltpu.roll(east_ref[species], to_last, 1),
                pltpu.roll(u, cols - 1, 1),
            )
            v_north = jnp.where(
                sub == rows - 1,
                north[pl.ds(species * levels + k, 1), :],
                pltpu.roll(v, rows - 1, 0),
            )
            from_west, to_west = jnp.maximum(u, 0.0), jnp.minimum(u, 0.0)
            to_east, from_east = jnp.maximum(u_east, 0.0), jnp.minimum(u_east, 0.0)
            from_south, to_south = jnp.maximum(v, 0.0), jnp.minimum(v, 0.0)
            to_north, from_north = jnp.maximum(v_north, 0.0), jnp.minimum(v_north, 0.0)
            stay = 1.0 - (to_east - to_west) - (to_north - to_south)
            for s in range(species):
                c = c_ref[s, k].astype(F32)
                c_west = jnp.where(
                    lane == 0, pltpu.roll(west_ref[s], to_first, 1), pltpu.roll(c, 1, 1)
                )
                c_east = jnp.where(
                    lane == cols - 1,
                    pltpu.roll(east_ref[s], to_last, 1),
                    pltpu.roll(c, cols - 1, 1),
                )
                c_south = jnp.where(
                    sub == 0, south[pl.ds(s * levels + k, 1), :], pltpu.roll(c, 1, 0)
                )
                c_north = jnp.where(
                    sub == rows - 1,
                    north[pl.ds(s * levels + k, 1), :],
                    pltpu.roll(c, rows - 1, 0),
                )
                value = (
                    stay * c
                    + (from_west * c_west - from_east * c_east)
                    + (from_south * c_south - from_north * c_north)
                ).astype(BF16)
                out_ref[s, k] = value
                tile = slice(s * rows, (s + 1) * rows)
                state[p, tile, lanes] = value.astype(F32)
                rate = table_ref[index_ref[s], k]
                loss[p, tile, lanes] = jnp.full((rows, cols), rate, F32)
                base[p, tile, lanes] = jnp.full((rows, cols), 1.0 + rate, F32)
        return 0

    lax.fori_loop(0, pairs, advect, 0)

    def substep(step, _):
        below = flux = None
        for p in range(pairs):
            q = state[p]
            high = q.astype(BF16)
            low = (q - high.astype(F32)).astype(BF16)
            made = jnp.dot(
                matrix[...],
                jnp.concatenate([high, low, high, low], axis=0),
                preferred_element_type=F32,
            )
            under = base[p] + loss[p] * (q * q)
            z = made * pl.reciprocal(under, approx=True)
            for half in range(2):
                k = 2 * p + half
                here = z[:, half * cols : (half + 1) * cols]
                if k > 0:
                    upward = kappa_ref[k - 1] * (here - below)
                    done = below + (upward if k == 1 else upward - flux)
                    lanes = slice((1 - half) * cols, (2 - half) * cols)
                    state[p + half - 1, :, lanes] = done
                    flux = upward
                below = here
        state[pairs - 1, :, cols:] = below - flux
        return 0

    lax.fori_loop(0, SUBSTEPS, substep, 0)

    lit = light_ref[...] > 0

    def finish(p, _):
        for half in range(2):
            k = 2 * p + half
            lanes = slice(half * cols, (half + 1) * cols)
            for s in range(species):
                done = state[p, s * rows : (s + 1) * rows, lanes]
                out_ref[s, k] = jnp.where(lit, done, out_ref[s, k].astype(F32)).astype(BF16)
        return 0

    lax.fori_loop(0, pairs, finish, 0)


def vmem():
    return pl.BlockSpec(memory_space=pltpu.VMEM)


def smem():
    return pl.BlockSpec(memory_space=pltpu.SMEM)


def solution(mesh):
    placed = (
        P(None, None, "lat", "lon"),
        P(None, "lat", "lon"),
        P(None, "lat", "lon"),
        P("lat", "lon"),
        P(),
        P(),
        P(),
        P(),
    )
    lon_count, lat_count = mesh.shape["lon"], mesh.shape["lat"]

    def local(tracers, east_wind, north_wind, sunlit, coupling, rate_table, rate_index, kappa):
        species, levels, rows, cols = tracers.shape
        mix = species * rows
        pairs = levels // 2

        def rims(*refs):
            return rims_kernel(lon_count, lat_count, *refs)

        sides = pl.pallas_call(
            rims,
            out_shape=(
                jax.ShapeDtypeStruct((species + 1, rows, cols), F32),
                jax.ShapeDtypeStruct((species + 1, rows, cols), F32),
                jax.ShapeDtypeStruct((species * levels, cols), BF16),
                jax.ShapeDtypeStruct(((species + 1) * levels, cols), BF16),
            ),
            in_specs=[vmem()] * 3,
            out_specs=(vmem(),) * 4,
            scratch_shapes=[
                pltpu.VMEM(((species + 1) * levels, rows, cols), F32),
                pltpu.VMEM((species + 1, rows, cols), F32),
                pltpu.VMEM((species + 1, rows, cols), F32),
                pltpu.VMEM((species * levels, cols), BF16),
                pltpu.VMEM(((species + 1) * levels, cols), BF16),
                pltpu.SemaphoreType.DMA((4,)),
                pltpu.SemaphoreType.DMA((4,)),
            ],
            compiler_params=pltpu.CompilerParams(
                collective_id=0, has_side_effects=True, vmem_limit_bytes=32 * 2**20
            ),
            name="rims",
        )(tracers, east_wind, north_wind)
        return pl.pallas_call(
            column_kernel,
            out_shape=jax.ShapeDtypeStruct(tracers.shape, BF16),
            in_specs=[smem()] * 4 + [vmem()] * 8,
            out_specs=vmem(),
            scratch_shapes=[
                pltpu.VMEM((pairs, mix, 2 * cols), F32),
                pltpu.VMEM((pairs, mix, 2 * cols), F32),
                pltpu.VMEM((pairs, mix, 2 * cols), F32),
                pltpu.VMEM((mix, 4 * mix), F32),
                pltpu.VMEM((mix, 4 * mix), BF16),
                pltpu.VMEM((species * levels, cols), F32),
                pltpu.VMEM(((species + 1) * levels, cols), F32),
            ],
            compiler_params=pltpu.CompilerParams(vmem_limit_bytes=40 * 2**20),
            name="columns",
        )(
            coupling,
            rate_table,
            rate_index,
            kappa,
            tracers,
            east_wind,
            north_wind,
            sunlit,
            *sides,
        )

    return jax.shard_map(
        local, mesh=mesh, in_specs=placed, out_specs=P(None, None, "lat", "lon"), check_vma=False
    )
```
